512 devices in a mesh: row: 16 (over y_lo, x, core), col: 32 (over y_hi, z).
Axes of the slice: x: 4, y: 8 (y_hi: 4, y_lo: 2; y = y_hi * 2 + y_lo), z: 8, core: 2. Of those that a mesh axis runs over, the one named last changes fastest.
Arguments:
- x_in: bfloat16 [512, 12288], P('row', 'col'), may hold values from -18 to 18
- query: bfloat16 [512, 12288], P(('row', 'col')), may hold values from -6 to 6
- latest_key_value: bfloat16 [512, 2, 1024], P(('row', 'col')), may hold values from -6 to 6
- key_value_cache: bfloat16 [512, 2, 256, 1024], P(('row', 'col')), may hold values from -6 to 6
- lengths: int32 [512], P(('row', 'col')), may hold values from 2 to 256, as said below
- o_weight: bfloat16 [12288, 12288], P('row', 'col'), may hold values from -127 to 127
- o_scale: float32 [12288], P('col'), may hold values from 0.00049430673 to 0.001977227
- ffn_gain: float32 [12288], P('col'), may hold values from 0.25 to 1.75
- gate_up_weight: bfloat16 [2, 12288, 18432], P(None, 'col', 'row'), may hold values from -127 to 127
- gate_up_scale: float32 [2, 18432], P(None, 'row'), may hold values from 6.178834e-05 to 0.00024715337
- down_weight: bfloat16 [18432, 12288], P('row', 'col'), may hold values from -127 to 127
- down_scale: float32 [12288], P('col'), may hold values from 0.00010089994 to 0.00040359976
Outputs:
- x_out: bfloat16 [512, 12288], P('row', 'col')
The draws below stay inside these ranges and needn't reach their ends.
Inputs may be any that keep to these rules, and one draw needn't show every extreme that they name: `lengths`: some row uses all 256 slots.
All inputs are finite; a program needn't handle non-finite values.
Results may differ from the reference program's by a relative error of at most 0.029.
Values may be sent and summed in bfloat16 or wider, within the bound.
No kernel may reach another device: no remote copies, remote signals or barrier semaphores. Data moves between devices by JAX's collectives and lax.ppermute only.
A program may use at most 64 MiB of HBM per device.

```python
import math
import jax
import jax.numpy as jnp
from jax import lax

D = 12288
QUERY_HEADS = 96
KEY_VALUE_HEADS = 8
HEAD_SIZE = 128
FF = 18432
CONTEXT_SLOTS = 256
DECODE_ROWS = 512
N_COL = 32


def attention_pair(key):
    query_key = jax.random.fold_in(key, 101)
    cached_key_rows = jax.random.fold_in(key, 102)
    query_rows = jax.random.truncated_normal(query_key, -6.0, 6.0, (DECODE_ROWS, QUERY_HEADS * HEAD_SIZE), jnp.float32)
    cache_pairs = jax.random.truncated_normal(cached_key_rows, -6.0, 6.0, (DECODE_ROWS, 2, CONTEXT_SLOTS, KEY_VALUE_HEADS * HEAD_SIZE), jnp.float32)
    return (query_rows, cache_pairs)


def draw_query(key, part):
    return attention_pair(key)[0].astype(jnp.bfloat16)


def draw_key_value_cache(key, part):
    return attention_pair(key)[1].astype(jnp.bfloat16)


def draw_x_in(key, part):
    key = jax.random.fold_in(key, 7)
    column = jnp.arange(D, dtype=jnp.float32) / D
    value_rows = jax.random.truncated_normal(key, -6.0, 6.0, (DECODE_ROWS, D), jnp.float32)
    scales = jnp.power(3.0, column)[None, :]
    return (value_rows * scales).astype(jnp.bfloat16)


def draw_lengths(key, part):
    key = jax.random.fold_in(key, 31)
    drawn = jax.random.randint(key, (DECODE_ROWS,), 2, CONTEXT_SLOTS + 1, dtype=jnp.int32)
    return drawn.at[0].set(CONTEXT_SLOTS)


def integer_weights(key, shape):
    return jax.random.randint(key, shape, -127, 128, dtype=jnp.int32).astype(jnp.float32).astype(jnp.bfloat16)


def draw_o_weight(key, part):
    key = jax.random.fold_in(key, 41)
    return integer_weights(key, (QUERY_HEADS * HEAD_SIZE, D))


def draw_gate_up_weight(key, part):
    key = jax.random.fold_in(key, 42)
    return integer_weights(key, (2, D, FF))


def draw_down_weight(key, part):
    key = jax.random.fold_in(key, 43)
    return integer_weights(key, (FF, D))


def level_of(stream_key, shape, shards, least, largest):
    loudness, own = 1.0, jax.random.fold_in(stream_key, 6)
    for axis_at, blocks in shards:
        steps = jnp.exp(jax.random.uniform(jax.random.fold_in(own, axis_at), (blocks,), jnp.float32, least / len(shards), largest / len(shards)))
        loudness = loudness * jnp.repeat(steps, shape[axis_at] // blocks).reshape([-1 if axis == axis_at else 1 for axis in range(len(shape))])
    return loudness


def noise(stream_key, dims, scale, most, split=(), held_as=jnp.bfloat16):
    loudness = level_of(stream_key, dims, split, -0.22, 0.18) if split else 1.0
    values = jax.random.normal(stream_key, dims, jnp.float32) * scale * loudness
    return jnp.minimum(jnp.maximum(values, -most), most).astype(held_as)


def setup_inputs(seed: int = 0) -> dict:
    key_of = jax.random.split(jax.random.key(seed), 13)
    return {
        "x_in": draw_x_in(jax.random.fold_in(key_of[12], 71), 0),
        "query": draw_query(jax.random.fold_in(key_of[12], 71), 0),
        "latest_key_value": noise(key_of[2], (DECODE_ROWS, 2, KEY_VALUE_HEADS * HEAD_SIZE), 1.0, 6.0, ((0, 512),)),
        "key_value_cache": draw_key_value_cache(jax.random.fold_in(key_of[12], 71), 0),
        "lengths": draw_lengths(jax.random.fold_in(key_of[12], 71), 0),
        "o_weight": draw_o_weight(jax.random.fold_in(key_of[12], 71), 0),
        "o_scale": jnp.clip(jnp.exp(math.log(0.001977227) - 1.3862944 * jax.random.uniform(key_of[6], (D,), jnp.float32) ** level_of(key_of[6], (D,), ((0, 32),), -0.2, 0.2)), 0.00049430673, 0.001977227),
        "ffn_gain": jnp.clip(1.0 + 0.15 * jax.random.normal(key_of[7], (D,), jnp.float32), 0.25, 1.75),
        "gate_up_weight": draw_gate_up_weight(jax.random.fold_in(key_of[12], 71), 0),
        "gate_up_scale": jnp.clip(jnp.exp(math.log(0.00024715337) - 1.3862944 * jax.random.uniform(key_of[9], (2, FF), jnp.float32) ** level_of(key_of[9], (2, FF), ((1, 16),), -0.2, 0.2)), 6.178834155434743e-05, 0.00024715337),
        "down_weight": draw_down_weight(jax.random.fold_in(key_of[12], 71), 0),
        "down_scale": jnp.clip(jnp.exp(math.log(0.00040359976) - 1.3862944 * jax.random.uniform(key_of[11], (D,), jnp.float32) ** level_of(key_of[11], (D,), ((0, 32),), -0.2, 0.2)), 0.00010089994, 0.00040359976),
    }


def attend(query, latest_key_value, key_value_cache, lengths):
    slot_count = query.shape[0]
    query_group = QUERY_HEADS // KEY_VALUE_HEADS
    scale = HEAD_SIZE ** (-0.5)
    query_rows = query.astype(jnp.float32).reshape(slot_count, KEY_VALUE_HEADS, query_group, HEAD_SIZE)
    key_rows = key_value_cache[:, 0].astype(jnp.float32).reshape(slot_count, CONTEXT_SLOTS, KEY_VALUE_HEADS, HEAD_SIZE)
    value_rows = key_value_cache[:, 1].astype(jnp.float32).reshape(slot_count, CONTEXT_SLOTS, KEY_VALUE_HEADS, HEAD_SIZE)
    latest_keys = latest_key_value[:, 0].astype(jnp.float32).reshape(slot_count, KEY_VALUE_HEADS, HEAD_SIZE)
    latest_values = latest_key_value[:, 1].astype(jnp.float32).reshape(slot_count, KEY_VALUE_HEADS, HEAD_SIZE)
    cached = jnp.einsum('akgd,apkd->akgp', query_rows, key_rows) * scale
    fresh = jnp.einsum('akgd,akd->akg', query_rows, latest_keys) * scale
    position = jnp.arange(CONTEXT_SLOTS, dtype=jnp.int32)
    valid = position[None, :] < lengths.astype(jnp.int32)[:, None]
    cached = jnp.where(valid[:, None, None, :], cached, -jnp.inf)
    top = jnp.maximum(lax.optimization_barrier(jnp.max(cached, axis=3)), fresh)
    weight_cached = jnp.exp(cached - top[..., None])
    weight_fresh = jnp.exp(fresh - top)
    total = lax.optimization_barrier(jnp.sum(weight_cached, axis=3)) + weight_fresh
    probs_cached = (weight_cached / total[..., None]).astype(jnp.bfloat16)
    probs_fresh = (weight_fresh / total).astype(jnp.bfloat16)
    mixed = jnp.einsum('akgp,apkd->akgd', probs_cached.astype(jnp.float32), value_rows)
    mixed = mixed + probs_fresh.astype(jnp.float32)[..., None] * latest_values[:, :, None, :]
    return mixed.reshape(slot_count, QUERY_HEADS * HEAD_SIZE).astype(jnp.bfloat16)

def single_row(items):
    row_query, row_kv, row_cache, row_length = items
    return attend(row_query[None], row_kv[None], row_cache[None], row_length[None])[0]

def unit_partials(normed, gate_up_weight):
    width = D // N_COL

    def step(total, index):
        start = (index * width).astype(jnp.int32)
        block = lax.dynamic_slice_in_dim(normed, start, width, 1)
        gate_block = lax.dynamic_slice_in_dim(gate_up_weight[0], start, width, 0)
        up_block = lax.dynamic_slice_in_dim(gate_up_weight[1], start, width, 0)
        part = jnp.stack([jnp.dot(block, gate_block, preferred_element_type=jnp.float32), jnp.dot(block, up_block, preferred_element_type=jnp.float32)])
        rounded = lax.optimization_barrier(part.astype(jnp.bfloat16)).astype(jnp.float32)
        return (total + rounded, None)
    empty = jnp.zeros((2, normed.shape[0], FF), jnp.float32)
    total, _ = lax.scan(step, empty, jnp.arange(N_COL, dtype=jnp.int32))
    return total

def reference(x_in, query, latest_key_value, key_value_cache, lengths, o_weight, o_scale, ffn_gain, gate_up_weight, gate_up_scale, down_weight, down_scale):
    attn = lax.map(single_row, (query, latest_key_value, key_value_cache, lengths))
    stream = x_in.astype(jnp.float32) + jnp.dot(attn, o_weight, preferred_element_type=jnp.float32) * o_scale
    mean_square = lax.optimization_barrier(jnp.mean(stream * stream, axis=1))
    normed = (stream * lax.rsqrt(mean_square + 1e-05)[:, None] * ffn_gain).astype(jnp.bfloat16)
    sums = unit_partials(normed, gate_up_weight)
    gate_part = sums[0] * gate_up_scale[0]
    up_part = sums[1] * gate_up_scale[1]
    hidden = (jax.nn.silu(gate_part) * up_part).astype(jnp.bfloat16)
    lowered = jnp.dot(hidden, down_weight, preferred_element_type=jnp.float32) * down_scale
    return (stream + lowered).astype(jnp.bfloat16)
```

```python
import jax
import jax.numpy as jnp
from jax import lax
from jax.sharding import Mesh
from jax.sharding import PartitionSpec as P

D = 12288
QUERY_HEADS = 96
KEY_VALUE_HEADS = 8
HEAD_SIZE = 128
CONTEXT_SLOTS = 256
UNITS = 1152
WIDTH = 384

ROWS = ("ylo", "x", "core")
COLS = ("b", "zl")
SIDE = ("zl", "ylo", "x")
bf16 = jnp.bfloat16
f32 = jnp.float32


def attend_local(query, latest_key_value, key_value_cache, lengths):
    slot_count = query.shape[0]
    query_group = QUERY_HEADS // KEY_VALUE_HEADS
    scale = HEAD_SIZE ** (-0.5)
    query_rows = query.reshape(slot_count, KEY_VALUE_HEADS, query_group, HEAD_SIZE)
    key_rows = key_value_cache[:, 0].reshape(slot_count, CONTEXT_SLOTS, KEY_VALUE_HEADS, HEAD_SIZE)
    value_rows = key_value_cache[:, 1].reshape(
        slot_count, CONTEXT_SLOTS, KEY_VALUE_HEADS, HEAD_SIZE
    )
    latest_keys = latest_key_value[:, 0].reshape(slot_count, KEY_VALUE_HEADS, HEAD_SIZE)
    latest_values = latest_key_value[:, 1].reshape(slot_count, KEY_VALUE_HEADS, HEAD_SIZE)
    cached = (
        jnp.einsum("akgd,apkd->akgp", query_rows, key_rows, preferred_element_type=jnp.float32)
        * scale
    )
    fresh = (
        jnp.einsum("akgd,akd->akg", query_rows, latest_keys, preferred_element_type=jnp.float32)
        * scale
    )
    position = jnp.arange(CONTEXT_SLOTS, dtype=jnp.int32)
    valid = position[None, :] < lengths[:, None]
    cached = jnp.where(valid[:, None, None, :], cached, -jnp.inf)
    top = jnp.maximum(jnp.max(cached, axis=3), fresh)
    weight_cached = jnp.exp(cached - top[..., None])
    weight_fresh = jnp.exp(fresh - top)
    total = jnp.sum(weight_cached, axis=3) + weight_fresh
    probs_cached = (weight_cached / total[..., None]).astype(jnp.bfloat16)
    probs_fresh = (weight_fresh / total).astype(jnp.bfloat16)
    mixed = jnp.einsum(
        "akgp,apkd->akgd", probs_cached, value_rows, preferred_element_type=jnp.float32
    )
    mixed = (
        mixed
        + probs_fresh.astype(jnp.float32)[..., None]
        * latest_values.astype(jnp.float32)[:, :, None, :]
    )
    return mixed.reshape(slot_count, QUERY_HEADS * HEAD_SIZE).astype(jnp.bfloat16)


def swap(block):
    return lax.ppermute(block, ("core", "zl"), [(0, 0), (1, 2), (2, 1), (3, 3)])


def both(block):
    return lax.all_gather(block, "core", axis=0, tiled=False)


def exchange(parts, axis):
    return lax.all_to_all(parts, axis, split_axis=0, concat_axis=0, tiled=False)


def spread(block, axis, count):
    return exchange(jnp.broadcast_to(block[None], (count,) + block.shape), axis)


def high_low(value):
    high = value.astype(bf16)
    low = (value - high.astype(f32)).astype(bf16)
    return high, low


def body(
    x_in,
    query,
    latest_key_value,
    key_value_cache,
    lengths,
    o_weight,
    o_scale,
    ffn_gain,
    gate_up_weight,
    gate_up_scale,
    down_weight,
    down_scale,
):
    scale_high, scale_low = high_low(gate_up_scale)
    gate_up_block = jnp.concatenate(
        [
            gate_up_weight.reshape(2 * WIDTH, UNITS),
            scale_high,
            scale_low,
            jnp.zeros((12, UNITS), bf16),
        ],
        axis=0,
    )
    o_blocks = both(swap(o_weight))
    gate_up_blocks = both(swap(gate_up_block))
    down_blocks = both(swap(down_weight))

    attn = attend_local(query, latest_key_value, key_value_cache, lengths)
    attn = attn.reshape(8, 2, 768).transpose(1, 0, 2).reshape(16, 768)
    attn = exchange(attn, SIDE)
    attn = spread(attn, "b", 16)
    attn = attn.reshape(16, 2, 8, 768).transpose(2, 0, 1, 3).reshape(256, 768)
    parts = jnp.einsum("mk,zkn->zmn", attn, o_blocks, preferred_element_type=f32).astype(bf16)
    parts = exchange(parts.reshape(16, 32, WIDTH), SIDE)
    attended = jnp.sum(parts.astype(f32), axis=0)
    stream = x_in.astype(f32) + attended * o_scale

    squares = jnp.sum(stream * stream, axis=1, keepdims=True)
    high, low = high_low(squares)
    lane = lax.broadcasted_iota(jnp.int32, (32, 128), 1)
    extra = jnp.where(lane == 0, high, jnp.where(lane == 1, low, jnp.zeros((), bf16)))
    gained = jnp.concatenate([(stream * ffn_gain).astype(bf16), extra], axis=1)
    gained = spread(gained, SIDE, 16).reshape(2, 256, WIDTH + 128)
    weights = gate_up_blocks[:, : 2 * WIDTH].reshape(2, 2, WIDTH, UNITS)
    partial_value = jnp.einsum(
        "zmd,zkdf->mkf", gained[:, :, :WIDTH], weights, preferred_element_type=f32
    )
    block_squares = jnp.sum(gained[:, :, WIDTH:].astype(f32), axis=(0, 2), keepdims=False)[:, None]
    high, low = high_low(block_squares)
    lane = lax.broadcasted_iota(jnp.int32, (256, 128), 1)
    extra = jnp.where(lane == 0, high, jnp.where(lane == 1, low, jnp.zeros((), bf16)))
    partial_value = jnp.concatenate(
        [partial_value.reshape(256, 2 * UNITS).astype(bf16), extra], axis=1
    )
    shares = exchange(partial_value.reshape(16, 16, 2 * UNITS + 128), "b")
    shares = jnp.sum(shares.astype(f32), axis=0)
    squares = jnp.sum(shares[:, 2 * UNITS :], axis=1, keepdims=True)
    inverse = lax.rsqrt(squares / D + 1e-05)
    scales = gate_up_blocks[0, 2 * WIDTH : 2 * WIDTH + 4].astype(f32)
    scales = scales[:2] + scales[2:]
    gate_part = shares[:, :UNITS] * inverse * scales[0]
    up_part = shares[:, UNITS : 2 * UNITS] * inverse * scales[1]
    hidden = (jax.nn.silu(gate_part) * up_part).astype(bf16)
    hidden = spread(hidden, "b", 16).reshape(256, UNITS)
    parts = jnp.einsum("mk,zkn->zmn", hidden, down_blocks, preferred_element_type=f32).astype(bf16)
    parts = exchange(parts.reshape(16, 32, WIDTH), SIDE)
    lowered = jnp.sum(parts.astype(f32), axis=0)
    return (stream + lowered * down_scale).astype(bf16)


def solution(mesh):
    mesh = Mesh(mesh.devices.reshape(2, 4, 2, 16, 2), ("ylo", "x", "core", "b", "zl"))
    everywhere = ROWS + COLS
    in_specs = (
        P(ROWS, COLS),
        P(everywhere, None),
        P(everywhere, None, None),
        P(everywhere, None, None, None),
        P(everywhere),
        P(ROWS, COLS),
        P(COLS),
        P(COLS),
        P(None, COLS, ROWS),
        P(None, ROWS),
        P(ROWS, COLS),
        P(COLS),
    )
    out_specs = P(ROWS, COLS)
    return jax.shard_map(body, mesh=mesh, in_specs=in_specs, out_specs=out_specs, check_vma=False)
```

```python
import jax
import jax.numpy as jnp
from jax import lax
from jax.experimental import pallas as pl
from jax.experimental.pallas import tpu as pltpu
from jax.sharding import Mesh
from jax.sharding import PartitionSpec as P

D = 12288
GROUPS = 8
GROUP_HEADS = 12
HEAD_SIZE = 128
CONTEXT_SLOTS = 256
UNITS = 1152
WIDTH = 384
EXTRA = 128
PACK_SCALES = 768
PACK_ROWS = 784

ROWS = ("ylo", "x", "core")
COLS = ("b", "zl")
NEAR = ("ylo", "x")
SIDE = ("zl", "ylo", "x")
bf16 = jnp.bfloat16
f32 = jnp.float32

VMEM = pl.BlockSpec(memory_space=pltpu.VMEM)
SMEM = pl.BlockSpec(memory_space=pltpu.SMEM)
HBM = pl.BlockSpec(memory_space=pltpu.HBM)
PARAMS = pltpu.CompilerParams(vmem_limit_bytes=32 * 1024 * 1024)


def dot(a, b):
    return jnp.dot(a, b, preferred_element_type=f32)


def high_low(value):
    high = value.astype(bf16).astype(f32)
    return high, value - high


def in_hbm(array):
    return pltpu.with_memory_space_constraint(array, pltpu.HBM)


def pack_kernel(weight_ref, scale_ref, gain_ref, out_ref, scale, gain, sems):
    copies = [
        pltpu.make_async_copy(scale_ref, scale, sems.at[0]),
        pltpu.make_async_copy(gain_ref, gain, sems.at[1]),
        pltpu.make_async_copy(weight_ref, out_ref.at[pl.ds(0, PACK_SCALES), :], sems.at[2]),
    ]
    for copy in copies:
        copy.start()
    copies[0].wait()
    copies[1].wait()
    rows = [
        part[k : k + 1, j * WIDTH : (j + 1) * WIDTH]
        for part in high_low(scale[...])
        for k in range(2)
        for j in range(3)
    ]
    rows.extend(high_low(gain[...].reshape(1, WIDTH)))
    rows.append(jnp.zeros((2, WIDTH), f32))
    out_ref[PACK_SCALES:, :] = jnp.concatenate(rows, axis=0).astype(bf16)
    copies[2].wait()


def pack(o_weight, gate_up_scale, ffn_gain):
    return pl.pallas_call(
        pack_kernel,
        out_shape=jax.ShapeDtypeStruct((PACK_ROWS, WIDTH), bf16),
        in_specs=[HBM, HBM, HBM],
        out_specs=VMEM,
        scratch_shapes=[
            pltpu.VMEM((2, UNITS), f32),
            pltpu.VMEM((WIDTH,), f32),
            pltpu.SemaphoreType.DMA((3,)),
        ],
        compiler_params=PARAMS,
        name="pack",
    )(in_hbm(o_weight), in_hbm(gate_up_scale), in_hbm(ffn_gain))


def attend_kernel(
    length_ref, query_in, latest_in, cache_ref, out_ref, query_row, latest_ref, query_ref, cache, sems
):
    small = [
        pltpu.make_async_copy(query_in, query_row, sems.at[2]),
        pltpu.make_async_copy(latest_in, latest_ref, sems.at[3]),
    ]
    for copy in small:
        copy.start()
    copies = [
        pltpu.make_async_copy(cache_ref.at[0, part], cache.at[part], sems.at[part])
        for part in range(2)
    ]
    for copy in copies:
        copy.start()
    for copy in small:
        copy.wait()
    for g in range(GROUPS):
        for h in range(GROUP_HEADS):
            at = (g * GROUP_HEADS + h) * HEAD_SIZE
            query_ref[g, h : h + 1] = query_row[:, at : at + HEAD_SIZE].astype(f32)
    scale = HEAD_SIZE ** (-0.5)
    slot = lax.broadcasted_iota(jnp.int32, (GROUP_HEADS, CONTEXT_SLOTS), 1)
    valid = slot < length_ref[0]
    lanes = [slice(g * HEAD_SIZE, (g + 1) * HEAD_SIZE) for g in range(GROUPS)]
    fresh = [
        jnp.sum(
            query_ref[g] * latest_ref[0, 0:1, lanes[g]].astype(f32),
            axis=1,
            keepdims=True,
        )
        * scale
        for g in range(GROUPS)
    ]
    copies[0].wait()
    cached = [
        jnp.where(
            valid,
            lax.dot_general(
                query_ref[g].astype(bf16),
                cache[0, :, lanes[g]],
                (((1,), (1,)), ((), ())),
                preferred_element_type=f32,
            )
            * scale,
            -jnp.inf,
        )
        for g in range(GROUPS)
    ]
    tops = [
        jnp.maximum(jnp.max(cached[g], axis=1, keepdims=True), fresh[g]) for g in range(GROUPS)
    ]
    weights = [jnp.exp(cached[g] - tops[g]) for g in range(GROUPS)]
    fresh = [jnp.exp(fresh[g] - tops[g]) for g in range(GROUPS)]
    inverse = [
        1.0 / (jnp.sum(weights[g], axis=1, keepdims=True) + fresh[g]) for g in range(GROUPS)
    ]
    probs = [(weights[g] * inverse[g]).astype(bf16) for g in range(GROUPS)]
    fresh = [(fresh[g] * inverse[g]).astype(bf16).astype(f32) for g in range(GROUPS)]
    copies[1].wait()
    mixed = [
        dot(probs[g], cache[1, :, lanes[g]])
        + fresh[g] * latest_ref[0, 1:2, lanes[g]].astype(f32)
        for g in range(GROUPS)
    ]
    for g in range(GROUPS):
        out_ref[g] = mixed[g].astype(bf16)


def attend(query, latest_key_value, key_value_cache, lengths):
    return pl.pallas_call(
        attend_kernel,
        out_shape=jax.ShapeDtypeStruct((GROUPS, GROUP_HEADS, HEAD_SIZE), bf16),
        in_specs=[SMEM, HBM, HBM, HBM],
        out_specs=VMEM,
        scratch_shapes=[
            pltpu.VMEM((1, D), bf16),
            pltpu.VMEM((1, 2, GROUPS * HEAD_SIZE), bf16),
            pltpu.VMEM((GROUPS, GROUP_HEADS, HEAD_SIZE), f32),
            pltpu.VMEM((2, CONTEXT_SLOTS, GROUPS * HEAD_SIZE), bf16),
            pltpu.SemaphoreType.DMA((4,)),
        ],
        compiler_params=PARAMS,
        name="attend",
    )(lengths, in_hbm(query), in_hbm(latest_key_value), in_hbm(key_value_cache))


def repeat_kernel(heads_ref, out_ref):
    half = GROUP_HEADS // 2
    for z in range(2):
        for j in range(half):
            block = heads_ref[:, z * half + j, :]
            for b in range(16):
                out_ref[2 * b + z, :, j * HEAD_SIZE : (j + 1) * HEAD_SIZE] = block


def repeat(heads):
    return pl.pallas_call(
        repeat_kernel,
        out_shape=jax.ShapeDtypeStruct((32, 8, 768), bf16),
        in_specs=[VMEM],
        out_specs=VMEM,
        compiler_params=PARAMS,
        name="repeat",
    )(heads)


def project_kernel(attn_ref, weight_ref, out_ref, weight, sems):
    copies = [
        pltpu.make_async_copy(
            weight_ref.at[z, pl.ds(0, PACK_SCALES), :], weight.at[z], sems.at[z]
        )
        for z in range(2)
    ]
    for copy in copies:
        copy.start()
    row = lax.broadcasted_iota(jnp.int32, (256, 256), 0)
    source = (row & 31) * 8 + (row >> 5)
    pick = (lax.broadcasted_iota(jnp.int32, (256, 256), 1) == source).astype(f32).astype(bf16)
    attn = attn_ref[...].astype(f32).reshape(256, 768).astype(bf16)
    attn = dot(pick, attn).astype(bf16)
    for z in range(2):
        copies[z].wait()
        out_ref[z] = dot(attn, weight[z]).astype(bf16)


def project(attn, weights):
    return pl.pallas_call(
        project_kernel,
        out_shape=jax.ShapeDtypeStruct((2, 256, WIDTH), bf16),
        in_specs=[VMEM, HBM],
        out_specs=VMEM,
        scratch_shapes=[pltpu.VMEM((2, 768, WIDTH), bf16), pltpu.SemaphoreType.DMA((2,))],
        compiler_params=PARAMS,
        name="project",
    )(attn, in_hbm(weights))


def stream_kernel(parts_ref, x_ref, scale_ref, gain_ref, stream_ref, out_ref):
    attended = parts_ref[0].astype(f32)
    for s in range(1, 16):
        attended = attended + parts_ref[s].astype(f32)
    stream = x_ref[...].astype(f32) + attended * scale_ref[...]
    stream_ref[...] = stream
    gained = (stream * gain_ref[...]).astype(bf16)
    for s in range(16):
        out_ref[s] = gained


def stream_and_spread(parts, x_in, o_scale, ffn_gain):
    return pl.pallas_call(
        stream_kernel,
        out_shape=(
            jax.ShapeDtypeStruct((32, WIDTH), f32),
            jax.ShapeDtypeStruct((16, 32, WIDTH), bf16),
        ),
        in_specs=[VMEM] * 4,
        out_specs=(VMEM, VMEM),
        compiler_params=PARAMS,
        name="stream",
    )(parts, x_in, o_scale[None], ffn_gain[None])


def gate_up_kernel(rows_ref, weight_ref, packed_ref, out_ref, weight, scales, sems, scale_sem):
    copies = [
        pltpu.make_async_copy(
            weight_ref.at[z, pl.ds(k * WIDTH, WIDTH), :],
            weight.at[k, pl.ds(z * WIDTH, WIDTH), :],
            sems.at[k, z],
        )
        for k in range(2)
        for z in range(2)
    ]
    scale_copy = pltpu.make_async_copy(
        packed_ref.at[:, pl.ds(PACK_SCALES, 16), :], scales, scale_sem.at[0]
    )
    for copy in copies:
        copy.start()
    scale_copy.start()
    rows = [rows_ref[z * 8 : z * 8 + 8].reshape(256, WIDTH) for z in range(2)]
    both_rows = jnp.concatenate(rows, axis=1)
    for k in range(2):
        copies[2 * k].wait()
        copies[2 * k + 1].wait()
        for j in range(3):
            column = (k * 3 + j) * WIDTH
            out_ref[:, column : column + WIDTH] = dot(
                both_rows, weight[k, :, j * WIDTH : (j + 1) * WIDTH]
            ).astype(bf16)
    scale_copy.wait()
    squares = jnp.zeros((256, 1), f32)
    for z in range(2):
        gain = scales[z].astype(f32)
        gain = gain[12:13] + gain[13:14]
        scaled = rows[z].astype(f32) * (1.0 / gain)
        squares = squares + jnp.sum(scaled * scaled, axis=1, keepdims=True)
    high, low = high_low(squares)
    lane = lax.broadcasted_iota(jnp.int32, (256, EXTRA), 1)
    out_ref[:, 2 * UNITS :] = jnp.where(
        lane == 0, high, jnp.where(lane == 1, low, 0.0)
    ).astype(bf16)


def gate_up(rows, weights, packed):
    return pl.pallas_call(
        gate_up_kernel,
        out_shape=jax.ShapeDtypeStruct((256, 2 * UNITS + EXTRA), bf16),
        in_specs=[VMEM, HBM, HBM],
        out_specs=VMEM,
        scratch_shapes=[
            pltpu.VMEM((2, 2 * WIDTH, UNITS), bf16),
            pltpu.VMEM((2, 16, WIDTH), bf16),
            pltpu.SemaphoreType.DMA((2, 2)),
            pltpu.SemaphoreType.DMA((1,)),
        ],
        compiler_params=PARAMS,
        name="gate_up",
    )(rows, in_hbm(weights), in_hbm(packed))


def hidden_kernel(shares_ref, packed_ref, out_ref, scale_rows, sem):
    copy = pltpu.make_async_copy(
        packed_ref.at[0, pl.ds(PACK_SCALES, 16), :], scale_rows, sem.at[0]
    )
    copy.start()
    extra = shares_ref[0, :, 2 * UNITS :].astype(f32)
    for s in range(1, 16):
        extra = extra + shares_ref[s, :, 2 * UNITS :].astype(f32)
    squares = jnp.sum(extra, axis=1, keepdims=True)
    inverse = lax.rsqrt(squares / D + 1e-05)
    copy.wait()
    scales = scale_rows[...].astype(f32)
    scales = scales[0:6] + scales[6:12]
    for j in range(3):
        parts = []
        for k in range(2):
            lanes = slice((k * 3 + j) * WIDTH, (k * 3 + j + 1) * WIDTH)
            total = shares_ref[0, :, lanes].astype(f32)
            for s in range(1, 16):
                total = total + shares_ref[s, :, lanes].astype(f32)
            parts.append(total * inverse * scales[k * 3 + j : k * 3 + j + 1])
        gate, up = parts
        hidden = (gate / (1.0 + jnp.exp(-gate)) * up).astype(bf16)
        for b in range(16):
            out_ref[b, :, j * WIDTH : (j + 1) * WIDTH] = hidden


def hidden_and_spread(shares, packed):
    return pl.pallas_call(
        hidden_kernel,
        out_shape=jax.ShapeDtypeStruct((16, 16, UNITS), bf16),
        in_specs=[VMEM, HBM],
        out_specs=VMEM,
        scratch_shapes=[pltpu.VMEM((16, WIDTH), bf16), pltpu.SemaphoreType.DMA((1,))],
        compiler_params=PARAMS,
        name="hidden",
    )(shares, in_hbm(packed))


def down_kernel(hidden_ref, weight_ref, out_ref, weight, sems):
    copies = [
        pltpu.make_async_copy(weight_ref.at[z], weight.at[z], sems.at[z]) for z in range(2)
    ]
    for copy in copies:
        copy.start()
    hidden = hidden_ref[...].reshape(256, UNITS)
    for z in range(2):
        copies[z].wait()
        out_ref[z] = dot(hidden, weight[z]).astype(bf16)


def down(hidden, weights):
    return pl.pallas_call(
        down_kernel,
        out_shape=jax.ShapeDtypeStruct((2, 256, WIDTH), bf16),
        in_specs=[VMEM, HBM],
        out_specs=VMEM,
        scratch_shapes=[pltpu.VMEM((2, UNITS, WIDTH), bf16), pltpu.SemaphoreType.DMA((2,))],
        compiler_params=PARAMS,
        name="down",
    )(hidden, in_hbm(weights))


def swap(block):
    return lax.ppermute(block, ("core", "zl"), [(0, 0), (1, 2), (2, 1), (3, 3)])


def both(block):
    return lax.all_gather(block, "core", axis=0, tiled=False)


def exchange(parts, axis):
    return lax.all_to_all(parts, axis, split_axis=0, concat_axis=0, tiled=False)


def body(
    x_in,
    query,
    latest_key_value,
    key_value_cache,
    lengths,
    o_weight,
    o_scale,
    ffn_gain,
    gate_up_weight,
    gate_up_scale,
    down_weight,
    down_scale,
):
    packed = swap(pack(o_weight, gate_up_scale, ffn_gain))
    gate_up_weight = swap(gate_up_weight.reshape(2 * WIDTH, UNITS))
    heads = attend(query, latest_key_value, key_value_cache, lengths)
    heads = exchange(heads, NEAR)
    heads, packed = lax.optimization_barrier((heads, packed))
    packed = both(packed)
    attn = exchange(repeat(heads), COLS)
    attn, gate_up_weight, down_weight = lax.optimization_barrier(
        (attn, gate_up_weight, down_weight)
    )
    gate_up_weight = both(gate_up_weight)
    down_weight = swap(down_weight)
    parts = exchange(project(attn, packed).reshape(16, 32, WIDTH), SIDE)
    stream, rows = stream_and_spread(parts, x_in, o_scale, ffn_gain)
    rows = exchange(rows, SIDE)
    rows, down_weight = lax.optimization_barrier((rows, down_weight))
    down_weight = both(down_weight)
    shares = exchange(
        gate_up(rows, gate_up_weight, packed).reshape(16, 16, 2 * UNITS + EXTRA), "b"
    )
    hidden = hidden_and_spread(shares, packed)
    hidden = exchange(hidden, "b")
    parts = exchange(down(hidden, down_weight).reshape(16, 32, WIDTH), SIDE)
    lowered = jnp.sum(parts.astype(f32), axis=0)
    return (stream + lowered * down_scale).astype(bf16)


def solution(mesh):
    mesh = Mesh(mesh.devices.reshape(2, 4, 2, 16, 2), ("ylo", "x", "core", "b", "zl"))
    everywhere = ROWS + COLS
    in_specs = (
        P(ROWS, COLS),
        P(everywhere, None),
        P(everywhere, None, None),
        P(everywhere, None, None, None),
        P(everywhere),
        P(ROWS, COLS),
        P(COLS),
        P(COLS),
        P(None, COLS, ROWS),
        P(None, ROWS),
        P(ROWS, COLS),
        P(COLS),
    )
    out_specs = P(ROWS, COLS)
    return jax.shard_map(body, mesh=mesh, in_specs=in_specs, out_specs=out_specs, check_vma=False)
```

```python
import jax
import jax.numpy as jnp
from jax import lax
from jax.experimental import pallas as pl
from jax.experimental.pallas import tpu as pltpu
from jax.sharding import Mesh
from jax.sharding import PartitionSpec as P

D = 12288
GROUPS = 8
GROUP_HEADS = 12
HEAD_SIZE = 128
CONTEXT_SLOTS = 256
UNITS = 1152
WIDTH = 384
EXTRA = 128
PACK_SCALES = 768
PACK_ROWS = 784

ROWS = ("ylo", "x", "core")
COLS = ("b", "zl")
NEAR = ("ylo", "x")
SIDE = ("zl", "ylo", "x")
bf16 = jnp.bfloat16
f32 = jnp.float32

VMEM = pl.BlockSpec(memory_space=pltpu.VMEM)
SMEM = pl.BlockSpec(memory_space=pltpu.SMEM)
HBM = pl.BlockSpec(memory_space=pltpu.HBM)
PARAMS = pltpu.CompilerParams(vmem_limit_bytes=10 * 1024 * 1024)


def dot(a, b):
    return jnp.dot(a, b, preferred_element_type=f32)


def high_low(value):
    high = value.astype(bf16).astype(f32)
    return high, value - high


def in_hbm(array):
    return pltpu.with_memory_space_constraint(array, pltpu.HBM)


def attend_kernel(
    length_ref,
    query_in,
    latest_in,
    cache_ref,
    gate_up_ref,
    scale_ref,
    gain_ref,
    out_ref,
    packed_ref,
    query_row,
    latest_ref,
    query_ref,
    cache,
    unit_scale,
    gain,
    sems,
):
    small = [
        pltpu.make_async_copy(query_in, query_row, sems.at[2]),
        pltpu.make_async_copy(latest_in, latest_ref, sems.at[3]),
    ]
    copies = [
        pltpu.make_async_copy(cache_ref.at[0, part], cache.at[part], sems.at[part])
        for part in range(2)
    ]
    packs = [
        pltpu.make_async_copy(scale_ref, unit_scale, sems.at[4]),
        pltpu.make_async_copy(gain_ref, gain, sems.at[5]),
        pltpu.make_async_copy(gate_up_ref, packed_ref.at[pl.ds(0, PACK_SCALES), :], sems.at[6]),
    ]
    for copy in small + copies + packs:
        copy.start()
    for copy in small:
        copy.wait()
    for g in range(GROUPS):
        for h in range(GROUP_HEADS):
            at = (g * GROUP_HEADS + h) * HEAD_SIZE
            query_ref[g, h : h + 1] = query_row[:, at : at + HEAD_SIZE].astype(f32)
    scale = HEAD_SIZE ** (-0.5)
    slot = lax.broadcasted_iota(jnp.int32, (GROUP_HEADS, CONTEXT_SLOTS), 1)
    valid = slot < length_ref[0]
    lanes = [slice(g * HEAD_SIZE, (g + 1) * HEAD_SIZE) for g in range(GROUPS)]
    fresh = [
        jnp.sum(
            query_ref[g] * latest_ref[0, 0:1, lanes[g]].astype(f32),
            axis=1,
            keepdims=True,
        )
        * scale
        for g in range(GROUPS)
    ]
    copies[0].wait()
    cached = [
        jnp.where(
            valid,
            lax.dot_general(
                query_ref[g].astype(bf16),
                cache[0, :, lanes[g]],
                (((1,), (1,)), ((), ())),
                preferred_element_type=f32,
            )
            * scale,
            -jnp.inf,
        )
        for g in range(GROUPS)
    ]
    tops = [
        jnp.maximum(jnp.max(cached[g], axis=1, keepdims=True), fresh[g]) for g in range(GROUPS)
    ]
    weights = [jnp.exp(cached[g] - tops[g]) for g in range(GROUPS)]
    fresh = [jnp.exp(fresh[g] - tops[g]) for g in range(GROUPS)]
    inverse = [
        1.0 / (jnp.sum(weights[g], axis=1, keepdims=True) + fresh[g]) for g in range(GROUPS)
    ]
    probs = [(weights[g] * inverse[g]).astype(bf16) for g in range(GROUPS)]
    fresh = [(fresh[g] * inverse[g]).astype(bf16).astype(f32) for g in range(GROUPS)]
    copies[1].wait()
    mixed = [
        dot(probs[g], cache[1, :, lanes[g]])
        + fresh[g] * latest_ref[0, 1:2, lanes[g]].astype(f32)
        for g in range(GROUPS)
    ]
    for g in range(GROUPS):
        out_ref[g] = mixed[g].astype(bf16)


    packs[0].wait()
    packs[1].wait()
    rows = list(high_low(unit_scale[...]))
    for part in high_low(gain[...].reshape(1, WIDTH)):
        rows.append(jnp.concatenate([part, jnp.zeros((1, UNITS - WIDTH), f32)], axis=1))
    rows.append(jnp.zeros((10, UNITS), f32))
    packed_ref[PACK_SCALES:, :] = jnp.concatenate(rows, axis=0).astype(bf16)
    packs[2].wait()


def attend(
    query, latest_key_value, key_value_cache, lengths, gate_up_weight, gate_up_scale, ffn_gain
):
    return pl.pallas_call(
        attend_kernel,
        out_shape=(
            jax.ShapeDtypeStruct((GROUPS, GROUP_HEADS, HEAD_SIZE), bf16),
            pltpu.VMEM((PACK_ROWS, UNITS), bf16),
        ),
        in_specs=[SMEM] + [HBM] * 6,
        out_specs=(VMEM, VMEM),
        scratch_shapes=[
            pltpu.VMEM((1, D), bf16),
            pltpu.VMEM((1, 2, GROUPS * HEAD_SIZE), bf16),
            pltpu.VMEM((GROUPS, GROUP_HEADS, HEAD_SIZE), f32),
            pltpu.VMEM((2, CONTEXT_SLOTS, GROUPS * HEAD_SIZE), bf16),
            pltpu.VMEM((2, UNITS), f32),
            pltpu.VMEM((WIDTH,), f32),
            pltpu.SemaphoreType.DMA((7,)),
        ],
        compiler_params=PARAMS,
        name="attend",
    )(
        lengths,
        in_hbm(query),
        in_hbm(latest_key_value),
        in_hbm(key_value_cache),
        in_hbm(gate_up_weight),
        in_hbm(gate_up_scale),
        in_hbm(ffn_gain),
    )


def repeat_kernel(heads_ref, out_ref):
    half = GROUP_HEADS // 2
    for z in range(2):
        for j in range(half):
            block = heads_ref[:, z * half + j, :]
            for b in range(16):
                out_ref[2 * b + z, :, j * HEAD_SIZE : (j + 1) * HEAD_SIZE] = block


def repeat(heads):
    return pl.pallas_call(
        repeat_kernel,
        out_shape=jax.ShapeDtypeStruct((32, 8, 768), bf16),
        in_specs=[VMEM],
        out_specs=VMEM,
        compiler_params=PARAMS,
        name="repeat",
    )(heads)


def project_kernel(attn_ref, own_ref, other_ref, out_ref):
    row = lax.broadcasted_iota(jnp.int32, (256, 256), 0)
    source = (row & 31) * 8 + (row >> 5)
    pick = (lax.broadcasted_iota(jnp.int32, (256, 256), 1) == source).astype(f32).astype(bf16)
    attn = attn_ref[...].astype(f32).reshape(256, 768).astype(bf16)
    attn = dot(pick, attn).astype(bf16)
    core = lax.axis_index("core")
    out_ref[core] = dot(attn, own_ref[...]).astype(bf16)
    out_ref[1 - core] = dot(attn, other_ref[...]).astype(bf16)


def project(attn, own, other):
    return pl.pallas_call(
        project_kernel,
        out_shape=jax.ShapeDtypeStruct((2, 256, WIDTH), bf16),
        in_specs=[VMEM, VMEM, VMEM],
        out_specs=VMEM,
        compiler_params=PARAMS,
        name="project",
    )(attn, own, other)


def stream_kernel(parts_ref, x_ref, scale_ref, gain_ref, stream_ref, out_ref):
    attended = parts_ref[0].astype(f32)
    for s in range(1, 16):
        attended = attended + parts_ref[s].astype(f32)
    stream = x_ref[...].astype(f32) + attended * scale_ref[...]
    stream_ref[...] = stream
    gained = (stream * gain_ref[...]).astype(bf16)
    for s in range(16):
        out_ref[s] = gained


def stream_and_spread(parts, x_in, o_scale, ffn_gain):
    return pl.pallas_call(
        stream_kernel,
        out_shape=(
            jax.ShapeDtypeStruct((32, WIDTH), f32),
            jax.ShapeDtypeStruct((16, 32, WIDTH), bf16),
        ),
        in_specs=[VMEM] * 4,
        out_specs=(VMEM, VMEM),
        compiler_params=PARAMS,
        name="stream",
    )(parts, x_in, o_scale[None], ffn_gain[None])


def stage(after, *arrays):
    count = len(arrays)

    def kernel(after_ref, *refs):
        sems = refs[-1]
        copies = [
            pltpu.make_async_copy(refs[n], refs[count + n], sems.at[n]) for n in range(count)
        ]
        for copy in copies:
            copy.start()
        for copy in copies:
            copy.wait()

    return pl.pallas_call(
        kernel,
        out_shape=[pltpu.VMEM(array.shape, array.dtype) for array in arrays],
        in_specs=[pl.BlockSpec(memory_space=pl.ANY)] + [HBM] * count,
        out_specs=[VMEM] * count,
        scratch_shapes=[pltpu.SemaphoreType.DMA((count,))],
        compiler_params=PARAMS,
        name="stage",
    )(after, *[in_hbm(array) for array in arrays])


def gate_up_kernel(rows_ref, own_ref, other_ref, out_ref):
    core = lax.axis_index("core")
    weights = (own_ref, other_ref)
    rows = [
        rows_ref[pl.ds(at * 8, 8)].reshape(256, WIDTH) for at in (core, 1 - core)
    ]
    both_rows = jnp.concatenate(rows, axis=1)
    for k in range(2):
        for at, size in ((0, 512), (512, 640)):
            weight = jnp.concatenate(
                [ref[k * WIDTH : (k + 1) * WIDTH, at : at + size] for ref in weights], axis=0
            )
            out_ref[:, k * UNITS + at : k * UNITS + at + size] = dot(both_rows, weight).astype(
                bf16
            )
    squares = jnp.zeros((256, 1), f32)
    for half in range(2):
        gain = weights[half][PACK_SCALES:, :WIDTH].astype(f32)
        gain = gain[4:5] + gain[5:6]
        scaled = rows[half].astype(f32) * (1.0 / gain)
        squares = squares + jnp.sum(scaled * scaled, axis=1, keepdims=True)
    high, low = high_low(squares)
    lane = lax.broadcasted_iota(jnp.int32, (256, EXTRA), 1)
    out_ref[:, 2 * UNITS :] = jnp.where(
        lane == 0, high, jnp.where(lane == 1, low, 0.0)
    ).astype(bf16)


def gate_up(rows, own, other):
    return pl.pallas_call(
        gate_up_kernel,
        out_shape=jax.ShapeDtypeStruct((256, 2 * UNITS + EXTRA), bf16),
        in_specs=[VMEM] * 3,
        out_specs=VMEM,
        compiler_params=PARAMS,
        name="gate_up",
    )(rows, own, other)


def hidden_kernel(shares_ref, scales_ref, out_ref):
    extra = shares_ref[0, :, 2 * UNITS :].astype(f32)
    for s in range(1, 16):
        extra = extra + shares_ref[s, :, 2 * UNITS :].astype(f32)
    squares = jnp.sum(extra, axis=1, keepdims=True)
    inverse = lax.rsqrt(squares / D + 1e-05)
    scales = scales_ref[...].astype(f32)
    scales = scales[0:2] + scales[2:4]
    for j in range(3):
        parts = []
        for k in range(2):
            lanes = slice((k * 3 + j) * WIDTH, (k * 3 + j + 1) * WIDTH)
            total = shares_ref[0, :, lanes].astype(f32)
            for s in range(1, 16):
                total = total + shares_ref[s, :, lanes].astype(f32)
            parts.append(total * inverse * scales[k : k + 1, j * WIDTH : (j + 1) * WIDTH])
        gate, up = parts
        hidden = (gate / (1.0 + jnp.exp(-gate)) * up).astype(bf16)
        for b in range(16):
            out_ref[b, :, j * WIDTH : (j + 1) * WIDTH] = hidden


def hidden_and_spread(shares, scales):
    return pl.pallas_call(
        hidden_kernel,
        out_shape=jax.ShapeDtypeStruct((16, 16, UNITS), bf16),
        in_specs=[VMEM, VMEM],
        out_specs=VMEM,
        compiler_params=PARAMS,
        name="hidden",
    )(shares, scales)


def down_kernel(hidden_ref, own_ref, other_ref, out_ref):
    core = lax.axis_index("core")
    hidden = hidden_ref[...].reshape(256, UNITS)
    out_ref[core] = dot(hidden, own_ref[...]).astype(bf16)
    out_ref[1 - core] = dot(hidden, other_ref[...]).astype(bf16)


def down(hidden, own, other):
    return pl.pallas_call(
        down_kernel,
        out_shape=jax.ShapeDtypeStruct((2, 256, WIDTH), bf16),
        in_specs=[VMEM, VMEM, VMEM],
        out_specs=VMEM,
        compiler_params=PARAMS,
        name="down",
    )(hidden, own, other)


def swap(block):
    return lax.ppermute(block, ("core", "zl"), [(0, 0), (1, 2), (2, 1), (3, 3)])


def other_core(block):
    return lax.ppermute(block, "core", [(0, 1), (1, 0)])


def exchange(parts, axis):
    return lax.all_to_all(parts, axis, split_axis=0, concat_axis=0, tiled=False)


def body(
    x_in,
    query,
    latest_key_value,
    key_value_cache,
    lengths,
    o_weight,
    o_scale,
    ffn_gain,
    gate_up_weight,
    gate_up_scale,
    down_weight,
    down_scale,
):
    own_o = swap(o_weight)
    heads, packed = attend(
        query,
        latest_key_value,
        key_value_cache,
        lengths,
        gate_up_weight.reshape(2 * WIDTH, UNITS),
        gate_up_scale,
        ffn_gain,
    )
    heads, own_o, packed = lax.optimization_barrier((heads, own_o, packed))
    other_o = other_core(own_o)
    own_gate_up = swap(packed)
    heads = exchange(heads, NEAR)
    attn = exchange(repeat(heads), COLS)
    attn, down_weight = lax.optimization_barrier((attn, down_weight))
    own_down = swap(down_weight)
    parts = project(attn, own_o, other_o)
    other_gate_up = other_core(own_gate_up)
    parts = exchange(parts.reshape(16, 32, WIDTH), SIDE)
    stream, rows = stream_and_spread(parts, x_in, o_scale, ffn_gain)
    (other_gate_up,) = stage(stream, other_gate_up)
    rows = exchange(rows, SIDE)
    rows, own_down = lax.optimization_barrier((rows, own_down))
    other_down = other_core(own_down)
    shares = exchange(
        gate_up(rows, own_gate_up, other_gate_up).reshape(16, 16, 2 * UNITS + EXTRA), "b"
    )
    hidden = hidden_and_spread(shares, own_gate_up[PACK_SCALES:])
    own_down, other_down = stage(hidden, own_down, other_down)
    hidden = exchange(hidden, "b")
    parts = exchange(down(hidden, own_down, other_down).reshape(16, 32, WIDTH), SIDE)
    lowered = jnp.sum(parts.astype(f32), axis=0)
    return (stream + lowered * down_scale).astype(bf16)


def solution(mesh):
    mesh = Mesh(mesh.devices.reshape(2, 4, 2, 16, 2), ("ylo", "x", "core", "b", "zl"))
    everywhere = ROWS + COLS
    in_specs = (
        P(ROWS, COLS),
        P(everywhere, None),
        P(everywhere, None, None),
        P(everywhere, None, None, None),
        P(everywhere),
        P(ROWS, COLS),
        P(COLS),
        P(COLS),
        P(None, COLS, ROWS),
        P(None, ROWS),
        P(ROWS, COLS),
        P(COLS),
    )
    out_specs = P(ROWS, COLS)
    return jax.shard_map(body, mesh=mesh, in_specs=in_specs, out_specs=out_specs, check_vma=False)
```

```python
import jax
import jax.numpy as jnp
from jax import lax
from jax.experimental import pallas as pl
from jax.experimental.pallas import tpu as pltpu
from jax.sharding import Mesh
from jax.sharding import PartitionSpec as P

D = 12288
GROUPS = 8
GROUP_HEADS = 12
HEAD_SIZE = 128
CONTEXT_SLOTS = 256
UNITS = 1152
WIDTH = 384
EXTRA = 128
PACK_SCALES = 768
PACK_ROWS = 784

ROWS = ("ylo", "x", "core")
COLS = ("b", "zl")
NEAR = ("ylo", "x")
SIDE = ("zl", "ylo", "x")
bf16 = jnp.bfloat16
f32 = jnp.float32

VMEM = pl.BlockSpec(memory_space=pltpu.VMEM)
SMEM = pl.BlockSpec(memory_space=pltpu.SMEM)
HBM = pl.BlockSpec(memory_space=pltpu.HBM)
PARAMS = pltpu.CompilerParams(vmem_limit_bytes=10 * 1024 * 1024)


def dot(a, b):
    return jnp.dot(a, b, preferred_element_type=f32)


def high_low(value):
    high = value.astype(bf16).astype(f32)
    return high, value - high


def in_hbm(array):
    return pltpu.with_memory_space_constraint(array, pltpu.HBM)


def attend_kernel(
    length_ref,
    query_in,
    latest_in,
    cache_ref,
    gate_up_ref,
    scale_ref,
    gain_ref,
    out_ref,
    packed_ref,
    query_row,
    latest_ref,
    query_ref,
    cache,
    unit_scale,
    gain,
    sems,
):
    small = [
        pltpu.make_async_copy(query_in, query_row, sems.at[2]),
        pltpu.make_async_copy(latest_in, latest_ref, sems.at[3]),
    ]
    copies = [
        pltpu.make_async_copy(cache_ref.at[0, part], cache.at[part], sems.at[part])
        for part in range(2)
    ]
    packs = [
        pltpu.make_async_copy(scale_ref, unit_scale, sems.at[4]),
        pltpu.make_async_copy(gain_ref, gain, sems.at[5]),
        pltpu.make_async_copy(gate_up_ref, packed_ref.at[pl.ds(0, PACK_SCALES), :], sems.at[6]),
    ]
    for copy in small + copies + packs:
        copy.start()
    for copy in small:
        copy.wait()
    for g in range(GROUPS):
        for h in range(GROUP_HEADS):
            at = (g * GROUP_HEADS + h) * HEAD_SIZE
            query_ref[g, h : h + 1] = query_row[:, at : at + HEAD_SIZE].astype(f32)
    scale = HEAD_SIZE ** (-0.5)
    slot = lax.broadcasted_iota(jnp.int32, (GROUP_HEADS, CONTEXT_SLOTS), 1)
    valid = slot < length_ref[0]
    lanes = [slice(g * HEAD_SIZE, (g + 1) * HEAD_SIZE) for g in range(GROUPS)]
    fresh = [
        jnp.sum(
            query_ref[g] * latest_ref[0, 0:1, lanes[g]].astype(f32),
            axis=1,
            keepdims=True,
        )
        * scale
        for g in range(GROUPS)
    ]
    copies[0].wait()
    cached = [
        jnp.where(
            valid,
            lax.dot_general(
                query_ref[g].astype(bf16),
                cache[0, :, lanes[g]],
                (((1,), (1,)), ((), ())),
                preferred_element_type=f32,
            )
            * scale,
            -jnp.inf,
        )
        for g in range(GROUPS)
    ]
    tops = [
        jnp.maximum(jnp.max(cached[g], axis=1, keepdims=True), fresh[g]) for g in range(GROUPS)
    ]
    weights = [jnp.exp(cached[g] - tops[g]) for g in range(GROUPS)]
    fresh = [jnp.exp(fresh[g] - tops[g]) for g in range(GROUPS)]
    inverse = [
        1.0 / (jnp.sum(weights[g], axis=1, keepdims=True) + fresh[g]) for g in range(GROUPS)
    ]
    probs = [(weights[g] * inverse[g]).astype(bf16) for g in range(GROUPS)]
    fresh = [(fresh[g] * inverse[g]).astype(bf16).astype(f32) for g in range(GROUPS)]
    copies[1].wait()
    mixed = [
        dot(probs[g], cache[1, :, lanes[g]])
        + fresh[g] * latest_ref[0, 1:2, lanes[g]].astype(f32)
        for g in range(GROUPS)
    ]
    for g in range(GROUPS):
        out_ref[g] = mixed[g].astype(bf16)


    packs[0].wait()
    packs[1].wait()
    rows = list(high_low(unit_scale[...]))
    for part in high_low(gain[...].reshape(1, WIDTH)):
        rows.append(jnp.concatenate([part, jnp.zeros((1, UNITS - WIDTH), f32)], axis=1))
    rows.append(jnp.zeros((10, UNITS), f32))
    packed_ref[PACK_SCALES:, :] = jnp.concatenate(rows, axis=0).astype(bf16)
    packs[2].wait()


def attend(
    query, latest_key_value, key_value_cache, lengths, gate_up_weight, gate_up_scale, ffn_gain
):
    return pl.pallas_call(
        attend_kernel,
        out_shape=(
            jax.ShapeDtypeStruct((GROUPS, GROUP_HEADS, HEAD_SIZE), bf16),
            pltpu.VMEM((PACK_ROWS, UNITS), bf16),
        ),
        in_specs=[SMEM] + [HBM] * 6,
        out_specs=(VMEM, VMEM),
        scratch_shapes=[
            pltpu.VMEM((1, D), bf16),
            pltpu.VMEM((1, 2, GROUPS * HEAD_SIZE), bf16),
            pltpu.VMEM((GROUPS, GROUP_HEADS, HEAD_SIZE), f32),
            pltpu.VMEM((2, CONTEXT_SLOTS, GROUPS * HEAD_SIZE), bf16),
            pltpu.VMEM((2, UNITS), f32),
            pltpu.VMEM((WIDTH,), f32),
            pltpu.SemaphoreType.DMA((7,)),
        ],
        compiler_params=PARAMS,
        name="attend",
    )(
        lengths,
        in_hbm(query),
        in_hbm(latest_key_value),
        in_hbm(key_value_cache),
        in_hbm(gate_up_weight),
        in_hbm(gate_up_scale),
        in_hbm(ffn_gain),
    )


def repeat_kernel(heads_ref, out_ref):
    half = GROUP_HEADS // 2
    for z in range(2):
        for j in range(half):
            block = heads_ref[:, z * half + j, :]
            for b in range(16):
                out_ref[2 * b + z, :, j * HEAD_SIZE : (j + 1) * HEAD_SIZE] = block


def repeat(heads):
    return pl.pallas_call(
        repeat_kernel,
        out_shape=jax.ShapeDtypeStruct((32, 8, 768), bf16),
        in_specs=[VMEM],
        out_specs=VMEM,
        compiler_params=PARAMS,
        name="repeat",
    )(heads)


def project_kernel(attn_ref, own_ref, other_in, out_ref, other_ref, sem):
    load = pltpu.make_async_copy(other_in, other_ref, sem.at[0])
    load.start()
    row = lax.broadcasted_iota(jnp.int32, (256, 256), 0)
    source = (row & 31) * 8 + (row >> 5)
    pick = (lax.broadcasted_iota(jnp.int32, (256, 256), 1) == source).astype(f32).astype(bf16)
    attn = attn_ref[...].astype(f32).reshape(256, 768).astype(bf16)
    attn = dot(pick, attn).astype(bf16)
    core = lax.axis_index("core")
    out_ref[core] = dot(attn, own_ref[...]).astype(bf16)
    load.wait()
    out_ref[1 - core] = dot(attn, other_ref[...]).astype(bf16)


def project(attn, own, other):
    return pl.pallas_call(
        project_kernel,
        out_shape=jax.ShapeDtypeStruct((2, 256, WIDTH), bf16),
        in_specs=[VMEM, VMEM, HBM],
        out_specs=VMEM,
        scratch_shapes=[pltpu.VMEM((768, WIDTH), bf16), pltpu.SemaphoreType.DMA((1,))],
        compiler_params=PARAMS,
        name="project",
    )(attn, own, in_hbm(other))


def stream_kernel(parts_ref, x_ref, scale_ref, gain_ref, stream_ref, out_ref):
    attended = parts_ref[0].astype(f32)
    for s in range(1, 16):
        attended = attended + parts_ref[s].astype(f32)
    stream = x_ref[...].astype(f32) + attended * scale_ref[...]
    stream_ref[...] = stream
    gained = (stream * gain_ref[...]).astype(bf16)
    for s in range(16):
        out_ref[s] = gained


def stream_and_spread(parts, x_in, o_scale, ffn_gain):
    return pl.pallas_call(
        stream_kernel,
        out_shape=(
            jax.ShapeDtypeStruct((32, WIDTH), f32),
            jax.ShapeDtypeStruct((16, 32, WIDTH), bf16),
        ),
        in_specs=[VMEM] * 4,
        out_specs=(VMEM, VMEM),
        compiler_params=PARAMS,
        name="stream",
    )(parts, x_in, o_scale[None], ffn_gain[None])


def stage(after, *arrays):
    count = len(arrays)

    def kernel(after_ref, *refs):
        sems = refs[-1]
        copies = [
            pltpu.make_async_copy(refs[n], refs[count + n], sems.at[n]) for n in range(count)
        ]
        for copy in copies:
            copy.start()
        for copy in copies:
            copy.wait()

    return pl.pallas_call(
        kernel,
        out_shape=[pltpu.VMEM(array.shape, array.dtype) for array in arrays],
        in_specs=[pl.BlockSpec(memory_space=pl.ANY)] + [HBM] * count,
        out_specs=[VMEM] * count,
        scratch_shapes=[pltpu.SemaphoreType.DMA((count,))],
        compiler_params=PARAMS,
        name="stage",
    )(after, *[in_hbm(array) for array in arrays])


def gate_up_kernel(rows_ref, own_ref, other_in, out_ref, other_ref, total, sems):
    cuts = ((PACK_SCALES, 16), (0, WIDTH), (WIDTH, WIDTH))
    loads = [
        pltpu.make_async_copy(
            other_in.at[pl.ds(at, size), :], other_ref.at[pl.ds(at, size), :], sems.at[n]
        )
        for n, (at, size) in enumerate(cuts)
    ]
    for load in loads:
        load.start()
    core = lax.axis_index("core")
    weights = (own_ref, other_ref)
    rows = [
        rows_ref[pl.ds(at * 8, 8)].reshape(256, WIDTH) for at in (core, 1 - core)
    ]
    both_rows = jnp.concatenate(rows, axis=1)
    total[...] = dot(rows[0], own_ref[:WIDTH])
    loads[0].wait()
    loads[1].wait()
    for at, size in ((0, 512), (512, 640)):
        out_ref[:, at : at + size] = (
            total[:, at : at + size] + dot(rows[1], other_ref[:WIDTH, at : at + size])
        ).astype(bf16)
    loads[2].wait()
    for at, size in ((0, 512), (512, 640)):
        weight = jnp.concatenate(
            [ref[WIDTH : 2 * WIDTH, at : at + size] for ref in weights], axis=0
        )
        out_ref[:, UNITS + at : UNITS + at + size] = dot(both_rows, weight).astype(bf16)
    squares = jnp.zeros((256, 1), f32)
    for half in range(2):
        gain = weights[half][PACK_SCALES:, :WIDTH].astype(f32)
        gain = gain[4:5] + gain[5:6]
        scaled = rows[half].astype(f32) * (1.0 / gain)
        squares = squares + jnp.sum(scaled * scaled, axis=1, keepdims=True)
    high, low = high_low(squares)
    lane = lax.broadcasted_iota(jnp.int32, (256, EXTRA), 1)
    out_ref[:, 2 * UNITS :] = jnp.where(
        lane == 0, high, jnp.where(lane == 1, low, 0.0)
    ).astype(bf16)


def gate_up(rows, own, other):
    return pl.pallas_call(
        gate_up_kernel,
        out_shape=jax.ShapeDtypeStruct((256, 2 * UNITS + EXTRA), bf16),
        in_specs=[VMEM, VMEM, HBM],
        out_specs=VMEM,
        scratch_shapes=[
            pltpu.VMEM((PACK_ROWS, UNITS), bf16),
            pltpu.VMEM((256, UNITS), f32),
            pltpu.SemaphoreType.DMA((3,)),
        ],
        compiler_params=PARAMS,
        name="gate_up",
    )(rows, own, in_hbm(other))


def hidden_kernel(shares_ref, scales_ref, out_ref):
    extra = shares_ref[0, :, 2 * UNITS :].astype(f32)
    for s in range(1, 16):
        extra = extra + shares_ref[s, :, 2 * UNITS :].astype(f32)
    squares = jnp.sum(extra, axis=1, keepdims=True)
    inverse = lax.rsqrt(squares / D + 1e-05)
    scales = scales_ref[...].astype(f32)
    scales = scales[0:2] + scales[2:4]
    for j in range(3):
        parts = []
        for k in range(2):
            lanes = slice((k * 3 + j) * WIDTH, (k * 3 + j + 1) * WIDTH)
            total = shares_ref[0, :, lanes].astype(f32)
            for s in range(1, 16):
                total = total + shares_ref[s, :, lanes].astype(f32)
            parts.append(total * inverse * scales[k : k + 1, j * WIDTH : (j + 1) * WIDTH])
        gate, up = parts
        hidden = (gate / (1.0 + jnp.exp(-gate)) * up).astype(bf16)
        for b in range(16):
            out_ref[b, :, j * WIDTH : (j + 1) * WIDTH] = hidden


def hidden_and_spread(shares, scales):
    return pl.pallas_call(
        hidden_kernel,
        out_shape=jax.ShapeDtypeStruct((16, 16, UNITS), bf16),
        in_specs=[VMEM, VMEM],
        out_specs=VMEM,
        compiler_params=PARAMS,
        name="hidden",
    )(shares, scales)


def down_kernel(hidden_ref, own_ref, other_ref, out_ref):
    core = lax.axis_index("core")
    hidden = hidden_ref[...].reshape(256, UNITS)
    out_ref[core] = dot(hidden, own_ref[...]).astype(bf16)
    out_ref[1 - core] = dot(hidden, other_ref[...]).astype(bf16)


def down(hidden, own, other):
    return pl.pallas_call(
        down_kernel,
        out_shape=jax.ShapeDtypeStruct((2, 256, WIDTH), bf16),
        in_specs=[VMEM, VMEM, VMEM],
        out_specs=VMEM,
        compiler_params=PARAMS,
        name="down",
    )(hidden, own, other)


def swap(block):
    return lax.ppermute(block, ("core", "zl"), [(0, 0), (1, 2), (2, 1), (3, 3)])


def other_core(block):
    return lax.ppermute(block, "core", [(0, 1), (1, 0)])


def exchange(parts, axis):
    return lax.all_to_all(parts, axis, split_axis=0, concat_axis=0, tiled=False)


def body(
    x_in,
    query,
    latest_key_value,
    key_value_cache,
    lengths,
    o_weight,
    o_scale,
    ffn_gain,
    gate_up_weight,
    gate_up_scale,
    down_weight,
    down_scale,
):
    own_o = swap(o_weight)
    heads, packed = attend(
        query,
        latest_key_value,
        key_value_cache,
        lengths,
        gate_up_weight.reshape(2 * WIDTH, UNITS),
        gate_up_scale,
        ffn_gain,
    )
    heads, own_o, packed = lax.optimization_barrier((heads, own_o, packed))
    other_o = other_core(own_o)
    own_gate_up = swap(packed)
    heads = exchange(heads, NEAR)
    repeated = repeat(heads)
    (down_weight,) = stage(repeated, down_weight)
    attn = exchange(repeated, COLS)
    attn, down_weight = lax.optimization_barrier((attn, down_weight))
    own_down = swap(down_weight)
    parts = project(attn, own_o, other_o)
    other_gate_up = other_core(own_gate_up)
    parts = exchange(parts.reshape(16, 32, WIDTH), SIDE)
    stream, rows = stream_and_spread(parts, x_in, o_scale, ffn_gain)
    rows = exchange(rows, SIDE)
    rows, own_down = lax.optimization_barrier((rows, own_down))
    other_down = other_core(own_down)
    shares = exchange(
        gate_up(rows, own_gate_up, other_gate_up).reshape(16, 16, 2 * UNITS + EXTRA), "b"
    )
    shares, other_down = lax.optimization_barrier((shares, other_down))
    hidden = hidden_and_spread(shares, own_gate_up[PACK_SCALES:])
    (own_down,) = stage(hidden, own_down)
    hidden = exchange(hidden, "b")
    parts = exchange(down(hidden, own_down, other_down).reshape(16, 32, WIDTH), SIDE)
    lowered = jnp.sum(parts.astype(f32), axis=0)
    return (stream + lowered * down_scale).astype(bf16)


def solution(mesh):
    mesh = Mesh(mesh.devices.reshape(2, 4, 2, 16, 2), ("ylo", "x", "core", "b", "zl"))
    everywhere = ROWS + COLS
    in_specs = (
        P(ROWS, COLS),
        P(everywhere, None),
        P(everywhere, None, None),
        P(everywhere, None, None, None),
        P(everywhere),
        P(ROWS, COLS),
        P(COLS),
        P(COLS),
        P(None, COLS, ROWS),
        P(None, ROWS),
        P(ROWS, COLS),
        P(COLS),
    )
    out_specs = P(ROWS, COLS)
    return jax.shard_map(body, mesh=mesh, in_specs=in_specs, out_specs=out_specs, check_vma=False)
```

```python
import jax
import jax.numpy as jnp
from jax import lax
from jax.experimental import pallas as pl
from jax.experimental.pallas import tpu as pltpu
from jax.sharding import Mesh
from jax.sharding import PartitionSpec as P

D = 12288
GROUPS = 8
GROUP_HEADS = 12
HEAD_SIZE = 128
CONTEXT_SLOTS = 256
UNITS = 1152
WIDTH = 384
EXTRA = 128
PACK_SCALES = 768
PACK_ROWS = 784

ROWS = ("ylo", "x", "core")
COLS = ("b", "zl")
NEAR = ("ylo", "x")
SIDE = ("zl", "ylo", "x")
bf16 = jnp.bfloat16
f32 = jnp.float32

VMEM = pl.BlockSpec(memory_space=pltpu.VMEM)
SMEM = pl.BlockSpec(memory_space=pltpu.SMEM)
HBM = pl.BlockSpec(memory_space=pltpu.HBM)
PARAMS = pltpu.CompilerParams(vmem_limit_bytes=10 * 1024 * 1024)


def dot(a, b):
    return jnp.dot(a, b, preferred_element_type=f32)


def high_low(value):
    high = value.astype(bf16).astype(f32)
    return high, value - high


def in_hbm(array):
    return pltpu.with_memory_space_constraint(array, pltpu.HBM)


def attend_kernel(
    length_ref,
    query_in,
    latest_in,
    cache_ref,
    gate_up_ref,
    scale_ref,
    gain_ref,
    out_ref,
    packed_ref,
    query_row,
    latest_ref,
    query_ref,
    cache,
    unit_scale,
    gain,
    sems,
):
    small = [
        pltpu.make_async_copy(query_in, query_row, sems.at[2]),
        pltpu.make_async_copy(latest_in, latest_ref, sems.at[3]),
    ]
    copies = [
        pltpu.make_async_copy(cache_ref.at[0, part], cache.at[part], sems.at[part])
        for part in range(2)
    ]
    packs = [
        pltpu.make_async_copy(scale_ref, unit_scale, sems.at[4]),
        pltpu.make_async_copy(gain_ref, gain, sems.at[5]),
        pltpu.make_async_copy(gate_up_ref, packed_ref.at[pl.ds(0, PACK_SCALES), :], sems.at[6]),
    ]
    for copy in small + copies + packs:
        copy.start()
    for copy in small:
        copy.wait()
    for g in range(GROUPS):
        for h in range(GROUP_HEADS):
            at = (g * GROUP_HEADS + h) * HEAD_SIZE
            query_ref[g, h : h + 1] = query_row[:, at : at + HEAD_SIZE].astype(f32)
    scale = HEAD_SIZE ** (-0.5)
    slot = lax.broadcasted_iota(jnp.int32, (GROUP_HEADS, CONTEXT_SLOTS), 1)
    valid = slot < length_ref[0]
    lanes = [slice(g * HEAD_SIZE, (g + 1) * HEAD_SIZE) for g in range(GROUPS)]
    fresh = [
        jnp.sum(
            query_ref[g] * latest_ref[0, 0:1, lanes[g]].astype(f32),
            axis=1,
            keepdims=True,
        )
        * scale
        for g in range(GROUPS)
    ]
    copies[0].wait()
    cached = [
        jnp.where(
            valid,
            lax.dot_general(
                query_ref[g].astype(bf16),
                cache[0, :, lanes[g]],
                (((1,), (1,)), ((), ())),
                preferred_element_type=f32,
            )
            * scale,
            -jnp.inf,
        )
        for g in range(GROUPS)
    ]
    tops = [
        jnp.maximum(jnp.max(cached[g], axis=1, keepdims=True), fresh[g]) for g in range(GROUPS)
    ]
    weights = [jnp.exp(cached[g] - tops[g]) for g in range(GROUPS)]
    fresh = [jnp.exp(fresh[g] - tops[g]) for g in range(GROUPS)]
    inverse = [
        1.0 / (jnp.sum(weights[g], axis=1, keepdims=True) + fresh[g]) for g in range(GROUPS)
    ]
    probs = [(weights[g] * inverse[g]).astype(bf16) for g in range(GROUPS)]
    fresh = [(fresh[g] * inverse[g]).astype(bf16).astype(f32) for g in range(GROUPS)]
    copies[1].wait()
    mixed = [
        dot(probs[g], cache[1, :, lanes[g]])
        + fresh[g] * latest_ref[0, 1:2, lanes[g]].astype(f32)
        for g in range(GROUPS)
    ]
    for g in range(GROUPS):
        out_ref[g] = mixed[g].astype(bf16)


    packs[0].wait()
    packs[1].wait()
    rows = list(high_low(unit_scale[...]))
    for part in high_low(gain[...].reshape(1, WIDTH)):
        rows.append(jnp.concatenate([part, jnp.zeros((1, UNITS - WIDTH), f32)], axis=1))
    rows.append(jnp.zeros((10, UNITS), f32))
    packed_ref[PACK_SCALES:, :] = jnp.concatenate(rows, axis=0).astype(bf16)
    packs[2].wait()


def attend(
    query, latest_key_value, key_value_cache, lengths, gate_up_weight, gate_up_scale, ffn_gain
):
    return pl.pallas_call(
        attend_kernel,
        out_shape=(
            jax.ShapeDtypeStruct((GROUPS, GROUP_HEADS, HEAD_SIZE), bf16),
            pltpu.VMEM((PACK_ROWS, UNITS), bf16),
        ),
        in_specs=[SMEM] + [HBM] * 6,
        out_specs=(VMEM, VMEM),
        scratch_shapes=[
            pltpu.VMEM((1, D), bf16),
            pltpu.VMEM((1, 2, GROUPS * HEAD_SIZE), bf16),
            pltpu.VMEM((GROUPS, GROUP_HEADS, HEAD_SIZE), f32),
            pltpu.VMEM((2, CONTEXT_SLOTS, GROUPS * HEAD_SIZE), bf16),
            pltpu.VMEM((2, UNITS), f32),
            pltpu.VMEM((WIDTH,), f32),
            pltpu.SemaphoreType.DMA((7,)),
        ],
        compiler_params=PARAMS,
        name="attend",
    )(
        lengths,
        in_hbm(query),
        in_hbm(latest_key_value),
        in_hbm(key_value_cache),
        in_hbm(gate_up_weight),
        in_hbm(gate_up_scale),
        in_hbm(ffn_gain),
    )


def repeat_kernel(heads_ref, out_ref):
    half = GROUP_HEADS // 2
    for z in range(2):
        for j in range(half):
            block = heads_ref[:, z * half + j, :]
            for b in range(16):
                out_ref[2 * b + z, :, j * HEAD_SIZE : (j + 1) * HEAD_SIZE] = block


def repeat(heads):
    return pl.pallas_call(
        repeat_kernel,
        out_shape=jax.ShapeDtypeStruct((32, 8, 768), bf16),
        in_specs=[VMEM],
        out_specs=VMEM,
        compiler_params=PARAMS,
        name="repeat",
    )(heads)


def project_kernel(attn_ref, own_in, other_in, out_ref, own_ref, other_ref, sems):
    loads = [
        pltpu.make_async_copy(own_in, own_ref, sems.at[0]),
        pltpu.make_async_copy(other_in, other_ref, sems.at[1]),
    ]
    for load in loads:
        load.start()
    row = lax.broadcasted_iota(jnp.int32, (256, 256), 0)
    source = (row & 31) * 8 + (row >> 5)
    pick = (lax.broadcasted_iota(jnp.int32, (256, 256), 1) == source).astype(f32).astype(bf16)
    attn = attn_ref[...].astype(f32).reshape(256, 768).astype(bf16)
    attn = dot(pick, attn).astype(bf16)
    core = lax.axis_index("core")
    loads[0].wait()
    out_ref[core] = dot(attn, own_ref[...]).astype(bf16)
    loads[1].wait()
    out_ref[1 - core] = dot(attn, other_ref[...]).astype(bf16)


def project(attn, own, other):
    return pl.pallas_call(
        project_kernel,
        out_shape=jax.ShapeDtypeStruct((2, 256, WIDTH), bf16),
        in_specs=[VMEM, HBM, HBM],
        out_specs=VMEM,
        scratch_shapes=[
            pltpu.VMEM((768, WIDTH), bf16),
            pltpu.VMEM((768, WIDTH), bf16),
            pltpu.SemaphoreType.DMA((2,)),
        ],
        compiler_params=PARAMS,
        name="project",
    )(attn, in_hbm(own), in_hbm(other))


def stream_kernel(parts_ref, x_ref, scale_ref, gain_ref, stream_ref, out_ref):
    attended = parts_ref[0].astype(f32)
    for s in range(1, 16):
        attended = attended + parts_ref[s].astype(f32)
    stream = x_ref[...].astype(f32) + attended * scale_ref[...]
    stream_ref[...] = stream
    gained = (stream * gain_ref[...]).astype(bf16)
    for s in range(16):
        out_ref[s] = gained


def stream_and_spread(parts, x_in, o_scale, ffn_gain):
    return pl.pallas_call(
        stream_kernel,
        out_shape=(
            jax.ShapeDtypeStruct((32, WIDTH), f32),
            jax.ShapeDtypeStruct((16, 32, WIDTH), bf16),
        ),
        in_specs=[VMEM] * 4,
        out_specs=(VMEM, VMEM),
        compiler_params=PARAMS,
        name="stream",
    )(parts, x_in, o_scale[None], ffn_gain[None])


def stage(after, *arrays):
    count = len(arrays)

    def kernel(after_ref, *refs):
        sems = refs[-1]
        copies = [
            pltpu.make_async_copy(refs[n], refs[count + n], sems.at[n]) for n in range(count)
        ]
        for copy in copies:
            copy.start()
        for copy in copies:
            copy.wait()

    return pl.pallas_call(
        kernel,
        out_shape=[pltpu.VMEM(array.shape, array.dtype) for array in arrays],
        in_specs=[pl.BlockSpec(memory_space=pl.ANY)] + [HBM] * count,
        out_specs=[VMEM] * count,
        scratch_shapes=[pltpu.SemaphoreType.DMA((count,))],
        compiler_params=PARAMS,
        name="stage",
    )(after, *[in_hbm(array) for array in arrays])


def gate_up_kernel(rows_ref, own_ref, other_in, out_ref, other_ref, total, sems):
    cuts = ((PACK_SCALES, 16), (0, WIDTH), (WIDTH, WIDTH))
    loads = [
        pltpu.make_async_copy(
            other_in.at[pl.ds(at, size), :], other_ref.at[pl.ds(at, size), :], sems.at[n]
        )
        for n, (at, size) in enumerate(cuts)
    ]
    for load in loads:
        load.start()
    core = lax.axis_index("core")
    weights = (own_ref, other_ref)
    rows = [
        rows_ref[pl.ds(at * 8, 8)].reshape(256, WIDTH) for at in (core, 1 - core)
    ]
    both_rows = jnp.concatenate(rows, axis=1)
    total[...] = dot(rows[0], own_ref[:WIDTH])
    loads[0].wait()
    loads[1].wait()
    for at, size in ((0, 512), (512, 640)):
        out_ref[:, at : at + size] = (
            total[:, at : at + size] + dot(rows[1], other_ref[:WIDTH, at : at + size])
        ).astype(bf16)
    loads[2].wait()
    for at, size in ((0, 512), (512, 640)):
        weight = jnp.concatenate(
            [ref[WIDTH : 2 * WIDTH, at : at + size] for ref in weights], axis=0
        )
        out_ref[:, UNITS + at : UNITS + at + size] = dot(both_rows, weight).astype(bf16)
    squares = jnp.zeros((256, 1), f32)
    for half in range(2):
        gain = weights[half][PACK_SCALES:, :WIDTH].astype(f32)
        gain = gain[4:5] + gain[5:6]
        scaled = rows[half].astype(f32) * (1.0 / gain)
        squares = squares + jnp.sum(scaled * scaled, axis=1, keepdims=True)
    high, low = high_low(squares)
    lane = lax.broadcasted_iota(jnp.int32, (256, EXTRA), 1)
    out_ref[:, 2 * UNITS :] = jnp.where(
        lane == 0, high, jnp.where(lane == 1, low, 0.0)
    ).astype(bf16)


def gate_up(rows, own, other):
    return pl.pallas_call(
        gate_up_kernel,
        out_shape=jax.ShapeDtypeStruct((256, 2 * UNITS + EXTRA), bf16),
        in_specs=[VMEM, VMEM, HBM],
        out_specs=VMEM,
        scratch_shapes=[
            pltpu.VMEM((PACK_ROWS, UNITS), bf16),
            pltpu.VMEM((256, UNITS), f32),
            pltpu.SemaphoreType.DMA((3,)),
        ],
        compiler_params=PARAMS,
        name="gate_up",
    )(rows, own, in_hbm(other))


def hidden_kernel(shares_ref, scales_ref, out_ref):
    extra = shares_ref[0, :, 2 * UNITS :].astype(f32)
    for s in range(1, 16):
        extra = extra + shares_ref[s, :, 2 * UNITS :].astype(f32)
    squares = jnp.sum(extra, axis=1, keepdims=True)
    inverse = lax.rsqrt(squares / D + 1e-05)
    scales = scales_ref[...].astype(f32)
    scales = scales[0:2] + scales[2:4]
    for j in range(3):
        parts = []
        for k in range(2):
            lanes = slice((k * 3 + j) * WIDTH, (k * 3 + j + 1) * WIDTH)
            total = shares_ref[0, :, lanes].astype(f32)
            for s in range(1, 16):
                total = total + shares_ref[s, :, lanes].astype(f32)
            parts.append(total * inverse * scales[k : k + 1, j * WIDTH : (j + 1) * WIDTH])
        gate, up = parts
        hidden = (gate / (1.0 + jnp.exp(-gate)) * up).astype(bf16)
        for b in range(16):
            out_ref[b, :, j * WIDTH : (j + 1) * WIDTH] = hidden


def hidden_and_spread(shares, scales):
    return pl.pallas_call(
        hidden_kernel,
        out_shape=jax.ShapeDtypeStruct((16, 16, UNITS), bf16),
        in_specs=[VMEM, VMEM],
        out_specs=VMEM,
        compiler_params=PARAMS,
        name="hidden",
    )(shares, scales)


def down_kernel(hidden_ref, own_ref, other_ref, out_ref):
    core = lax.axis_index("core")
    hidden = hidden_ref[...].reshape(256, UNITS)
    out_ref[core] = dot(hidden, own_ref[...]).astype(bf16)
    out_ref[1 - core] = dot(hidden, other_ref[...]).astype(bf16)


def down(hidden, own, other):
    return pl.pallas_call(
        down_kernel,
        out_shape=jax.ShapeDtypeStruct((2, 256, WIDTH), bf16),
        in_specs=[VMEM, VMEM, VMEM],
        out_specs=VMEM,
        compiler_params=PARAMS,
        name="down",
    )(hidden, own, other)


def swap(block):
    return lax.ppermute(block, ("core", "zl"), [(0, 0), (1, 2), (2, 1), (3, 3)])


def other_core(block):
    return lax.ppermute(block, "core", [(0, 1), (1, 0)])


def exchange(parts, axis):
    return lax.all_to_all(parts, axis, split_axis=0, concat_axis=0, tiled=False)


def body(
    x_in,
    query,
    latest_key_value,
    key_value_cache,
    lengths,
    o_weight,
    o_scale,
    ffn_gain,
    gate_up_weight,
    gate_up_scale,
    down_weight,
    down_scale,
):
    (o_weight,) = stage(in_hbm(key_value_cache), o_weight)
    own_o = swap(o_weight)
    heads, packed = attend(
        query,
        latest_key_value,
        key_value_cache,
        lengths,
        gate_up_weight.reshape(2 * WIDTH, UNITS),
        gate_up_scale,
        ffn_gain,
    )
    heads, own_o, packed = lax.optimization_barrier((heads, own_o, packed))
    other_o = other_core(own_o)
    own_gate_up = swap(packed)
    heads = exchange(heads, NEAR)
    repeated = repeat(heads)
    (down_weight,) = stage(repeated, down_weight)
    attn = exchange(repeated, COLS)
    attn, down_weight = lax.optimization_barrier((attn, down_weight))
    own_down = swap(down_weight)
    parts = project(attn, own_o, other_o)
    other_gate_up = other_core(own_gate_up)
    parts = exchange(parts.reshape(16, 32, WIDTH), SIDE)
    stream, rows = stream_and_spread(parts, x_in, o_scale, ffn_gain)
    rows = exchange(rows, SIDE)
    rows, own_down = lax.optimization_barrier((rows, own_down))
    other_down = other_core(own_down)
    shares = exchange(
        gate_up(rows, own_gate_up, other_gate_up).reshape(16, 16, 2 * UNITS + EXTRA), "b"
    )
    shares, other_down = lax.optimization_barrier((shares, other_down))
    hidden = hidden_and_spread(shares, own_gate_up[PACK_SCALES:])
    (own_down,) = stage(hidden, own_down)
    hidden = exchange(hidden, "b")
    parts = exchange(down(hidden, own_down, other_down).reshape(16, 32, WIDTH), SIDE)
    lowered = jnp.sum(parts.astype(f32), axis=0)
    return (stream + lowered * down_scale).astype(bf16)


def solution(mesh):
    mesh = Mesh(mesh.devices.reshape(2, 4, 2, 16, 2), ("ylo", "x", "core", "b", "zl"))
    everywhere = ROWS + COLS
    in_specs = (
        P(ROWS, COLS),
        P(everywhere, None),
        P(everywhere, None, None),
        P(everywhere, None, None, None),
        P(everywhere),
        P(ROWS, COLS),
        P(COLS),
        P(COLS),
        P(None, COLS, ROWS),
        P(None, ROWS),
        P(ROWS, COLS),
        P(COLS),
    )
    out_specs = P(ROWS, COLS)
    return jax.shard_map(body, mesh=mesh, in_specs=in_specs, out_specs=out_specs, check_vma=False)
```
